32 devices in a mesh: dp: 16 (over z, x, core), tensor: 2 (over y).
Axes of the slice: x: 2, y: 2, z: 4, core: 2. Of those that a mesh axis runs over, the one named last changes fastest.
Arguments:
- tokens: bfloat16 [768, 2048], P(('dp', 'tensor')), may hold values from -6 to 6
- grad_hidden: bfloat16 [768, 5504], P('dp', 'tensor'), may hold values from -0.21875 to 0.21875
- width_in: bfloat16 [2048, 1024], P(None, 'tensor'), may hold values from -0.125 to 0.125
- gate_small: bfloat16 [1024, 2752], P(None, 'tensor'), may hold values from -0.1875 to 0.1875
- up_small: bfloat16 [1024, 2752], P(None, 'tensor'), may hold values from -0.1875 to 0.1875
- width_hidden: bfloat16 [5504, 2752], P('tensor'), may hold values from -0.109375 to 0.109375
Outputs:
- grad_width_in: float32 [2048, 1024], P('dp', 'tensor')
- grad_gate_small: float32 [1024, 2752], P('dp', 'tensor')
- grad_up_small: float32 [1024, 2752], P('dp', 'tensor')
- grad_width_hidden: float32 [5504, 2752], P('tensor', 'dp')
The draws below stay inside these ranges and needn't reach their ends.
All inputs are finite; a program needn't handle non-finite values.
Results may differ from the reference program's by a relative error of at most 0.0085.
Values may be sent and summed in bfloat16 or wider, within the bound.
A program may use at most 128 MiB of HBM per device.

```python
import jax
import jax.numpy as jnp

D = 2048
DS = 1024
FS = 2752
FF = 5504
TOKENS = 768


def shard_levels(rng, dims, shards, least, high):
    loudness = 1.0
    for position, parts in shards:
        steps = jax.random.uniform(jax.random.fold_in(jax.random.fold_in(rng, 6), position), (parts,), jnp.float32, least / len(shards), high / len(shards))
        loudness = loudness * jnp.repeat(jnp.exp(steps), dims[position] // parts).reshape((-1,) + (1,) * (len(dims) - 1 - position))
    return loudness


def noise(key, shape, deviation, bound, split=(), held_as=jnp.bfloat16):
    entries = deviation * jax.random.normal(key, shape, jnp.float32)
    if split:
        entries = entries * shard_levels(key, shape, split, -0.22, 0.18)
    return jnp.clip(entries, -bound, bound).astype(held_as)


def setup_inputs(seed: int = 0) -> dict:
    arg_keys = jax.random.split(jax.random.key(seed), 7)
    return {
        "tokens": noise(arg_keys[0], (TOKENS, D), 1.0, 6.0, ((0, 32),)),
        "grad_hidden": noise(arg_keys[1], (TOKENS, FF), (TOKENS ** -0.5), 0.21875, ((0, 16), (1, 2))),
        "width_in": noise(arg_keys[2], (D, DS), D ** -0.5, 0.125, ((1, 2),)),
        "gate_small": noise(arg_keys[3], (DS, FS), DS ** -0.5, 0.1875, ((1, 2),)),
        "up_small": noise(arg_keys[4], (DS, FS), DS ** -0.5, 0.1875, ((1, 2),)),
        "width_hidden": noise(arg_keys[5], (FF, FS), FS ** -0.5, 0.109375, ((0, 2),)),
    }


def reference(tokens, grad_hidden, width_in, gate_small, up_small, width_hidden):
    narrow = jnp.dot(tokens, width_in, preferred_element_type=jnp.float32).astype(jnp.bfloat16)
    gate_low = jnp.dot(narrow, gate_small, preferred_element_type=jnp.float32).astype(jnp.bfloat16)
    up_low = jnp.dot(narrow, up_small, preferred_element_type=jnp.float32).astype(jnp.bfloat16)
    gate_big = jnp.dot(gate_low, width_hidden.T, preferred_element_type=jnp.float32)
    up_big = jnp.dot(up_low, width_hidden.T, preferred_element_type=jnp.float32)
    upstream = grad_hidden.astype(jnp.float32)
    sig = jax.nn.sigmoid(gate_big)
    d_gate = (upstream * up_big * sig * (1.0 + gate_big * (1.0 - sig))).astype(jnp.bfloat16)
    d_up = (upstream * gate_big * sig).astype(jnp.bfloat16)
    grad_width_hidden = jnp.dot(d_gate.T, gate_low, preferred_element_type=jnp.float32) + jnp.dot(d_up.T, up_low, preferred_element_type=jnp.float32)
    d_gate_low = jnp.dot(d_gate, width_hidden, preferred_element_type=jnp.float32).astype(jnp.bfloat16)
    d_up_low = jnp.dot(d_up, width_hidden, preferred_element_type=jnp.float32).astype(jnp.bfloat16)
    grad_gate_small = jnp.dot(narrow.T, d_gate_low, preferred_element_type=jnp.float32)
    grad_up_small = jnp.dot(narrow.T, d_up_low, preferred_element_type=jnp.float32)
    d_narrow = (jnp.dot(d_gate_low, gate_small.T, preferred_element_type=jnp.float32) + jnp.dot(d_up_low, up_small.T, preferred_element_type=jnp.float32)).astype(jnp.bfloat16)
    grad_width_in = jnp.dot(tokens.T, d_narrow, preferred_element_type=jnp.float32)
    return (grad_width_in, grad_gate_small, grad_up_small, grad_width_hidden)
```

```python
import functools

import jax
import jax.numpy as jnp
from jax import lax
from jax.experimental import pallas as pl
from jax.experimental.pallas import tpu as pltpu
from jax.sharding import PartitionSpec as P

BF = jnp.bfloat16
F32 = jnp.float32


def up_to(value, unit):
    return -(-value // unit) * unit


def fit(x, shape):
    return jnp.pad(x, [(0, want - have) for want, have in zip(shape, x.shape)])


def greet(n_dp, n_tp, dp, tp):
    barrier = pltpu.get_barrier_semaphore()
    for dt in range(n_tp):
        other = lax.rem(tp + dt, n_tp)

        def signal(k, carry, other=other):
            pl.semaphore_signal(
                barrier,
                inc=1,
                device_id=(lax.rem(dp + k, n_dp), other),
                device_id_type=pl.DeviceIdType.MESH,
            )
            return carry

        lax.fori_loop(1 if dt == 0 else 0, n_dp, signal, 0)
    pl.semaphore_wait(barrier, n_dp * n_tp - 1)


def spread(n_dp, n_tp, dp, tp, make, keep):
    keep.start()
    for act in ("start", "wait"):
        for dt in range(n_tp):
            other = lax.rem(tp + dt, n_tp)
            came = lax.rem(tp - dt + n_tp, n_tp)

            def step(k, carry, other=other, came=came, act=act):
                to = lax.rem(dp + k, n_dp)
                frm = lax.rem(dp - k + n_dp, n_dp)
                if act == "start":
                    for copy in make(to, other, dp, tp, dt):
                        copy.start()
                else:
                    for copy in make(to, other, frm, came, dt):
                        copy.wait()
                return carry

            lax.fori_loop(1 if dt == 0 else 0, n_dp, step, 0)
    keep.wait()


def first_exchange(n_dp, n_tp, d_ref, low_ref, tok_ref, d_out, low_out, tok_out,
                   d_s, d_r, low_s, low_r, tok_s, tok_r, own):
    dp, tp = lax.axis_index("dp"), lax.axis_index("tensor")
    greet(n_dp, n_tp, dp, tp)
    mesh_id = pl.DeviceIdType.MESH

    def copies(to, other, frm, came, dt):
        out = [pltpu.make_async_remote_copy(
            d_ref.at[to], d_out.at[came, frm], d_s.at[other, to], d_r.at[came, frm],
            device_id=(to, other), device_id_type=mesh_id)]
        if dt == 0:
            out.append(pltpu.make_async_remote_copy(
                low_ref.at[to], low_out.at[frm], low_s.at[to], low_r.at[frm],
                device_id=(to, other), device_id_type=mesh_id))
            out.append(pltpu.make_async_remote_copy(
                tok_ref.at[to], tok_out.at[frm], tok_s.at[to], tok_r.at[frm],
                device_id=(to, other), device_id_type=mesh_id))
        return out

    class Own:
        def __init__(self):
            self.all = [
                pltpu.make_async_copy(d_ref.at[dp], d_out.at[tp, dp], own.at[0]),
                pltpu.make_async_copy(low_ref.at[dp], low_out.at[dp], own.at[1]),
                pltpu.make_async_copy(tok_ref.at[dp], tok_out.at[dp], own.at[2]),
            ]

        def start(self):
            for copy in self.all:
                copy.start()

        def wait(self):
            for copy in self.all:
                copy.wait()

    spread(n_dp, n_tp, dp, tp, copies, Own())


def second_exchange(n_dp, n_tp, big_ref, small_ref, big_out, small_out,
                    big_s, big_r, small_s, small_r, own):
    dp, tp = lax.axis_index("dp"), lax.axis_index("tensor")
    greet(n_dp, n_tp, dp, tp)
    mesh_id = pl.DeviceIdType.MESH
    group = n_dp // n_tp
    home = lax.div(dp, group)

    def big_copy(m, t, slot):
        return pltpu.make_async_remote_copy(
            big_ref.at[m, t], big_out.at[slot], big_s.at[m, t], big_r.at[slot],
            device_id=(tp * group + m, t), device_id_type=mesh_id)

    def small_copy(to, slot):
        return pltpu.make_async_remote_copy(
            small_ref.at[to], small_out.at[slot], small_s.at[to], small_r.at[slot],
            device_id=(to, tp), device_id_type=mesh_id)

    my_m = lax.rem(dp, group)
    keep_small = pltpu.make_async_copy(small_ref.at[dp], small_out.at[dp], own.at[0])
    keep_small.start()
    keep_big = pltpu.make_async_copy(big_ref.at[my_m, tp], big_out.at[dp], own.at[1])

    @pl.when(home == tp)
    def _():
        keep_big.start()

    def send_big(n, carry):
        m, t = lax.rem(lax.rem(dp, group) + lax.div(n, n_tp), group), lax.rem(tp + n, n_tp)

        @pl.when(jnp.logical_or(tp * group + m != dp, t != tp))
        def _():
            big_copy(m, t, dp).start()

        return carry

    lax.fori_loop(0, n_dp, send_big, 0)

    def send_small(k, carry):
        small_copy(lax.rem(dp + k, n_dp), dp).start()
        return carry

    lax.fori_loop(1, n_dp, send_small, 0)

    def end_big(n, carry):
        m, t = lax.rem(lax.rem(dp, group) + lax.div(n, n_tp), group), lax.rem(tp + n, n_tp)

        @pl.when(jnp.logical_or(tp * group + m != dp, t != tp))
        def _():
            big_copy(m, t, dp).wait_send()

        @pl.when(jnp.logical_or(n != dp, home != tp))
        def _():
            big_copy(0, 0, n).wait_recv()

        return carry

    lax.fori_loop(0, n_dp, end_big, 0)

    def end_small(k, carry):
        small_copy(lax.rem(dp + k, n_dp), dp).wait_send()
        small_copy(dp, lax.rem(dp - k + n_dp, n_dp)).wait_recv()
        return carry

    lax.fori_loop(1, n_dp, end_small, 0)
    keep_small.wait()

    @pl.when(home == tp)
    def _():
        keep_big.wait()


ANY = pl.BlockSpec(memory_space=pl.ANY)


def exchange(kernel, collective_id, operands, out_shapes, sems):
    return pl.pallas_call(
        kernel,
        out_shape=out_shapes,
        in_specs=[ANY] * len(operands),
        out_specs=[ANY] * len(out_shapes),
        scratch_shapes=[pltpu.SemaphoreType.DMA(s) for s in sems],
        compiler_params=pltpu.CompilerParams(collective_id=collective_id, has_side_effects=True),
    )(*operands)


def contract_rows(left, right):
    return lax.dot_general(
        left, right, (((0,), (0,)), ((), ())), preferred_element_type=F32
    )


def contract_cols(left, right):
    return lax.dot_general(
        left, right, (((1,), (1,)), ((), ())), preferred_element_type=F32
    )


def on_device(n_dp, n_tp, tokens, grad_hidden, width_in, gate_small, up_small, width_hidden):
    rows = grad_hidden.shape[0]
    feats = tokens.shape[1]
    small = gate_small.shape[0]
    ff_part, fs = width_hidden.shape
    fs_part = gate_small.shape[1]
    fs_own = fs // n_dp
    group = n_dp // n_tp
    ff_blk = -(-ff_part // n_dp)
    fs_blk = -(-fs_part // n_dp)

    all_tokens = lax.all_gather(tokens, "tensor", axis=0, tiled=True)
    narrow_part = jnp.dot(all_tokens, width_in, preferred_element_type=F32).astype(BF)
    narrow = lax.all_gather(narrow_part, "tensor", axis=1, tiled=True)
    every_narrow = lax.all_gather(narrow, "dp", axis=0, tiled=True)
    gate_part = jnp.dot(narrow, gate_small, preferred_element_type=F32).astype(BF)
    up_part = jnp.dot(narrow, up_small, preferred_element_type=F32).astype(BF)
    low = lax.all_gather(
        jnp.concatenate([gate_part, up_part], axis=0), "tensor", axis=1, tiled=True
    )
    big = contract_cols(low, width_hidden)
    gate_big, up_big = big[:rows], big[rows:]
    upstream = grad_hidden.astype(F32)
    sig = jax.nn.sigmoid(gate_big)
    d_gate = (upstream * up_big * sig * (1.0 + gate_big * (1.0 - sig))).astype(BF)
    d_up = (upstream * gate_big * sig).astype(BF)

    back = jnp.dot(jnp.concatenate([d_gate, d_up], axis=0), width_hidden,
                   preferred_element_type=F32)
    d_low = lax.psum_scatter(back, "tensor", scatter_dimension=1, tiled=True).astype(BF)
    d_gate_low, d_up_low = d_low[:rows], d_low[rows:]
    narrow_back = contract_cols(d_gate_low, gate_small) + contract_cols(d_up_low, up_small)
    d_narrow = lax.psum_scatter(narrow_back, "tensor", scatter_dimension=1, tiled=True).astype(BF)
    every_d_narrow = lax.all_gather(d_narrow, "dp", axis=0, tiled=True)

    def blocks(gate, up, width):
        gate, up = (
            fit(part, (rows, n_dp * width)).reshape(rows, n_dp, width) for part in (gate, up)
        )
        both = jnp.concatenate([gate, up], axis=2).transpose(1, 0, 2)
        return fit(both, (n_dp, rows, up_to(2 * width, 128)))

    d_send = blocks(d_gate, d_up, ff_blk)
    low_send = blocks(d_gate_low, d_up_low, fs_blk)
    tok_send = all_tokens.reshape(rows, n_dp, feats // n_dp).transpose(1, 0, 2)
    d_got, low_got, tok_got = exchange(
        functools.partial(first_exchange, n_dp, n_tp),
        0,
        (d_send, low_send, tok_send),
        [
            jax.ShapeDtypeStruct((n_tp,) + d_send.shape, BF),
            jax.ShapeDtypeStruct(low_send.shape, BF),
            jax.ShapeDtypeStruct(tok_send.shape, BF),
        ],
        [(n_tp, n_dp), (n_tp, n_dp), (n_dp,), (n_dp,), (n_dp,), (n_dp,), (3,)],
    )

    count = n_dp * rows
    every_gate_low = jnp.dot(every_narrow, gate_small, preferred_element_type=F32).astype(BF)
    every_up_low = jnp.dot(every_narrow, up_small, preferred_element_type=F32).astype(BF)
    d_all = d_got.reshape(n_tp, count, -1)

    def hidden(d, low_all):
        return jnp.einsum("tkr,kc->trc", d, low_all, preferred_element_type=F32)

    term = hidden(d_all[:, :, :ff_blk], every_gate_low) + hidden(
        d_all[:, :, ff_blk : 2 * ff_blk], every_up_low
    )
    term = term.astype(BF).reshape(n_tp, ff_blk, group, fs_own).transpose(2, 0, 1, 3)
    big_send = fit(term, (group, n_tp, up_to(ff_blk, 16), up_to(fs_own, 128)))

    small_term = contract_rows(every_narrow, low_got.reshape(count, -1)).astype(BF)
    small_send = small_term.reshape(n_dp, small // n_dp, -1)
    big_got, small_got = exchange(
        functools.partial(second_exchange, n_dp, n_tp),
        1,
        (big_send, small_send),
        [
            jax.ShapeDtypeStruct((n_dp,) + big_send.shape[2:], BF),
            jax.ShapeDtypeStruct(small_send.shape, BF),
        ],
        [(group, n_tp), (n_dp,), (n_dp,), (n_dp,), (2,)],
    )
    grad_width_hidden = (
        big_got[:, :ff_blk, :fs_own].reshape(n_dp * ff_blk, fs_own)[:ff_part].astype(F32)
    )

    def small_out(start):
        part = small_got[:, :, start : start + fs_blk].transpose(1, 0, 2)
        return part.reshape(small // n_dp, n_dp * fs_blk)[:, :fs_part].astype(F32)

    grad_width_in = contract_rows(tok_got.reshape(count, -1), every_d_narrow)
    return (grad_width_in, small_out(0), small_out(fs_blk), grad_width_hidden)


def solution(mesh):
    return jax.shard_map(
        functools.partial(on_device, mesh.shape["dp"], mesh.shape["tensor"]),
        mesh=mesh,
        in_specs=(
            P(("dp", "tensor"), None),
            P("dp", "tensor"),
            P(None, "tensor"),
            P(None, "tensor"),
            P(None, "tensor"),
            P("tensor", None),
        ),
        out_specs=(P("dp", "tensor"), P("dp", "tensor"), P("dp", "tensor"), P("tensor", "dp")),
        check_vma=False,
    )
```

```python
import functools

import jax
import jax.numpy as jnp
from jax import lax
from jax.experimental import pallas as pl
from jax.experimental.pallas import tpu as pltpu
from jax.sharding import PartitionSpec as P

BF = jnp.bfloat16
F32 = jnp.float32


def up_to(value, unit):
    return -(-value // unit) * unit


def fit(x, shape):
    return jnp.pad(x, [(0, want - have) for want, have in zip(shape, x.shape)])


def greet(n_dp, n_tp, dp, tp):
    barrier = pltpu.get_barrier_semaphore()
    for dt in range(n_tp):
        other = lax.rem(tp + dt, n_tp)

        def signal(k, carry, other=other):
            pl.semaphore_signal(
                barrier,
                inc=1,
                device_id=(lax.rem(dp + k, n_dp), other),
                device_id_type=pl.DeviceIdType.MESH,
            )
            return carry

        lax.fori_loop(1 if dt == 0 else 0, n_dp, signal, 0)
    pl.semaphore_wait(barrier, n_dp * n_tp - 1)


def remote(src, dst, send_sem, recv_sem, dp, tp):
    return pltpu.make_async_remote_copy(
        src, dst, send_sem, recv_sem,
        device_id=(dp, tp), device_id_type=pl.DeviceIdType.MESH)


def first_exchange(n_dp, n_tp, d_ref, low_ref, tok_ref, d_out, low_out, tok_out,
                   d_s, d_r, pass_s, low_s, low_r, tok_s, tok_r, own):
    dp, tp = lax.axis_index("dp"), lax.axis_index("tensor")
    greet(n_dp, n_tp, dp, tp)

    def d_copy(to, frm):
        return remote(d_ref.at[to], d_out.at[tp, frm], d_s.at[to], d_r.at[tp, frm], to, tp)

    def pass_copy(frm, here, there):
        return remote(d_out.at[here, frm], d_out.at[here, frm], pass_s.at[there, frm],
                      d_r.at[here, frm], dp, there)

    def low_copy(to, frm):
        return remote(low_ref.at[to], low_out.at[frm], low_s.at[to], low_r.at[frm], to, tp)

    def tok_copy(to, frm):
        return remote(tok_ref.at[to], tok_out.at[frm], tok_s.at[to], tok_r.at[frm], to, tp)

    keep = [
        pltpu.make_async_copy(d_ref.at[dp], d_out.at[tp, dp], own.at[0]),
        pltpu.make_async_copy(low_ref.at[dp], low_out.at[dp], own.at[1]),
        pltpu.make_async_copy(tok_ref.at[dp], tok_out.at[dp], own.at[2]),
    ]
    for copy in keep:
        copy.start()

    def send(k, carry):
        d_copy(lax.rem(dp + k, n_dp), dp).start()
        return carry

    def send_rest(k, carry):
        low_copy(lax.rem(dp + k, n_dp), dp).start()
        tok_copy(lax.rem(dp + k, n_dp), dp).start()
        return carry

    lax.fori_loop(1, n_dp, send, 0)
    keep[0].wait()
    for dt in range(1, n_tp):
        pass_copy(dp, tp, lax.rem(tp + dt, n_tp)).start()
    lax.fori_loop(1, n_dp, send_rest, 0)

    def pass_on(k, carry):
        frm = lax.rem(dp - k + n_dp, n_dp)
        d_copy(dp, frm).wait_recv()
        for dt in range(1, n_tp):
            pass_copy(frm, tp, lax.rem(tp + dt, n_tp)).start()
        return carry

    lax.fori_loop(1, n_dp, pass_on, 0)

    def end(k, carry):
        to, frm = lax.rem(dp + k, n_dp), lax.rem(dp - k + n_dp, n_dp)
        d_copy(to, dp).wait_send()
        low_copy(to, dp).wait_send()
        low_copy(dp, frm).wait_recv()
        tok_copy(to, dp).wait_send()
        tok_copy(dp, frm).wait_recv()
        return carry

    lax.fori_loop(1, n_dp, end, 0)

    def end_pass(k, carry):
        frm = lax.rem(dp - k + n_dp, n_dp)
        for dt in range(1, n_tp):
            pass_copy(frm, tp, lax.rem(tp + dt, n_tp)).wait_send()
            pass_copy(frm, lax.rem(tp - dt + n_tp, n_tp), tp).wait_recv()
        return carry

    lax.fori_loop(0, n_dp, end_pass, 0)
    keep[1].wait()
    keep[2].wait()


def second_exchange(n_dp, n_tp, big_ref, small_ref, big_out, small_out, stage,
                    st_s, st_r, big_s, big_r, small_s, small_r, own):
    dp, tp = lax.axis_index("dp"), lax.axis_index("tensor")
    greet(n_dp, n_tp, dp, tp)
    group = n_dp // n_tp

    def stage_copy(t, u, m):
        return remote(big_ref.at[t, m], stage.at[u, m], st_s.at[t, m], st_r.at[u, m], dp, t)

    def big_copy(src, to, frm):
        return remote(src, big_out.at[frm], big_s.at[to], big_r.at[frm], to, tp)

    def small_copy(to, frm):
        return remote(small_ref.at[to], small_out.at[frm], small_s.at[to], small_r.at[frm], to, tp)

    def deliver(src, to):
        @pl.when(to != dp)
        def _():
            big_copy(src, to, dp).start()

        @pl.when(to == dp)
        def _():
            pltpu.make_async_copy(src, big_out.at[dp], own.at[1]).start()

    def nth(n):
        return lax.rem(dp + n, group)

    keep_small = pltpu.make_async_copy(small_ref.at[dp], small_out.at[dp], own.at[0])
    keep_small.start()

    def send(n, carry):
        m = nth(n)
        for dt in range(1, n_tp):
            stage_copy(lax.rem(tp + dt, n_tp), tp, m).start()
        deliver(big_ref.at[tp, m], tp * group + m)
        return carry

    lax.fori_loop(0, group, send, 0)

    def forward(n, carry):
        m = nth(n)
        for dt in range(1, n_tp):
            u = lax.rem(tp - dt + n_tp, n_tp)
            stage_copy(tp, u, m).wait_recv()
            deliver(stage.at[u, m], u * group + m)
        return carry

    lax.fori_loop(0, group, forward, 0)

    def send_small(k, carry):
        small_copy(lax.rem(dp + k, n_dp), dp).start()
        return carry

    lax.fori_loop(1, n_dp, send_small, 0)

    def end_stage(n, carry):
        for dt in range(1, n_tp):
            stage_copy(lax.rem(tp + dt, n_tp), tp, nth(n)).wait_send()
        return carry

    lax.fori_loop(0, group, end_stage, 0)

    def end(k, carry):
        to, frm = lax.rem(dp + k, n_dp), lax.rem(dp - k + n_dp, n_dp)
        big_copy(big_ref.at[0, 0], to, dp).wait_send()
        big_copy(big_ref.at[0, 0], dp, frm).wait_recv()
        small_copy(to, dp).wait_send()
        small_copy(dp, frm).wait_recv()
        return carry

    lax.fori_loop(1, n_dp, end, 0)
    keep_small.wait()
    pltpu.make_async_copy(big_ref.at[0, 0], big_out.at[dp], own.at[1]).wait()


ANY = pl.BlockSpec(memory_space=pl.ANY)


def exchange(kernel, collective_id, operands, out_shapes, sems):
    return pl.pallas_call(
        kernel,
        out_shape=out_shapes,
        in_specs=[ANY] * len(operands),
        out_specs=[ANY] * len(out_shapes),
        scratch_shapes=[pltpu.SemaphoreType.DMA(s) for s in sems],
        compiler_params=pltpu.CompilerParams(collective_id=collective_id, has_side_effects=True),
        cost_estimate=pl.CostEstimate(flops=0, bytes_accessed=120_000_000, transcendentals=0),
    )(*operands)


def gather_dp(x, n_dp):
    if n_dp & (n_dp - 1):
        return lax.all_gather(x, "dp", axis=0, tiled=True)
    dp = lax.axis_index("dp")
    held, place, step = x, 0, n_dp // 2
    while step:
        got = lax.ppermute(held, "dp", [(i, i ^ step) for i in range(n_dp)])
        low = lax.rem(lax.div(dp, step), 2) == 0
        held = jnp.stack([jnp.where(low, held, got), jnp.where(low, got, held)], axis=place)
        place, step = place + 1, step // 2
    return held.reshape((n_dp * x.shape[0],) + x.shape[1:])


def sum_tensor(x, n_tp):
    tp, width = lax.axis_index("tensor"), x.shape[1] // n_tp
    total = lax.dynamic_slice_in_dim(x, tp * width, width, 1)
    for hop in range(1, n_tp):
        term = lax.dynamic_slice_in_dim(x, lax.rem(tp + hop, n_tp) * width, width, 1)
        perm = [(t, (t + hop) % n_tp) for t in range(n_tp)]
        total = total + lax.ppermute(term.astype(BF), "tensor", perm).astype(F32)
    return total


def contract_rows(left, right):
    return lax.dot_general(
        left, right, (((0,), (0,)), ((), ())), preferred_element_type=F32
    )


def contract_cols(left, right):
    return lax.dot_general(
        left, right, (((1,), (1,)), ((), ())), preferred_element_type=F32
    )


def on_device(n_dp, n_tp, tokens, grad_hidden, width_in, gate_small, up_small, width_hidden):
    rows = grad_hidden.shape[0]
    feats = tokens.shape[1]
    small = gate_small.shape[0]
    ff_part, fs = width_hidden.shape
    fs_part = gate_small.shape[1]
    fs_own = fs // n_dp
    group = n_dp // n_tp
    ff_blk = up_to(-(-ff_part // n_dp), 16)
    fs_blk = -(-fs_part // n_dp)

    all_tokens = lax.all_gather(tokens, "tensor", axis=0, tiled=True)
    narrow_part = jnp.dot(all_tokens, width_in, preferred_element_type=F32).astype(BF)
    narrow = lax.all_gather(narrow_part, "tensor", axis=1, tiled=True)
    every_narrow = gather_dp(narrow, n_dp)
    gate_part = jnp.dot(narrow, gate_small, preferred_element_type=F32).astype(BF)
    up_part = jnp.dot(narrow, up_small, preferred_element_type=F32).astype(BF)
    low = lax.all_gather(
        jnp.concatenate([gate_part, up_part], axis=0), "tensor", axis=1, tiled=True
    )
    big = contract_cols(low, width_hidden)
    gate_big, up_big = big[:rows], big[rows:]
    upstream = grad_hidden.astype(F32)
    sig = jax.nn.sigmoid(gate_big)
    d_gate = (upstream * up_big * sig * (1.0 + gate_big * (1.0 - sig))).astype(BF)
    d_up = (upstream * gate_big * sig).astype(BF)

    back = jnp.dot(jnp.concatenate([d_gate, d_up], axis=0), width_hidden,
                   preferred_element_type=F32)
    d_low = sum_tensor(back, n_tp).astype(BF)
    d_gate_low, d_up_low = d_low[:rows], d_low[rows:]
    narrow_back = contract_cols(d_gate_low, gate_small) + contract_cols(d_up_low, up_small)
    d_narrow = sum_tensor(narrow_back, n_tp).astype(BF)
    every_d_narrow = gather_dp(d_narrow, n_dp)

    def blocks(gate, up, width):
        gate, up = (
            fit(part, (rows, n_dp * width)).reshape(rows, n_dp, width) for part in (gate, up)
        )
        both = jnp.concatenate([gate, up], axis=2).transpose(1, 0, 2)
        return fit(both, (n_dp, rows, up_to(2 * width, 128)))

    d_send = blocks(d_gate, d_up, ff_blk)
    low_send = blocks(d_gate_low, d_up_low, fs_blk)
    tok_send = all_tokens.reshape(rows, n_dp, feats // n_dp).transpose(1, 0, 2)
    d_got, low_got, tok_got = exchange(
        functools.partial(first_exchange, n_dp, n_tp),
        0,
        (d_send, low_send, tok_send),
        [
            jax.ShapeDtypeStruct((n_tp,) + d_send.shape, BF),
            jax.ShapeDtypeStruct(low_send.shape, BF),
            jax.ShapeDtypeStruct(tok_send.shape, BF),
        ],
        [(n_dp,), (n_tp, n_dp), (n_tp, n_dp), (n_dp,), (n_dp,), (n_dp,), (n_dp,), (3,)],
    )

    count = n_dp * rows
    every_gate_low = jnp.dot(every_narrow, gate_small, preferred_element_type=F32).astype(BF)
    every_up_low = jnp.dot(every_narrow, up_small, preferred_element_type=F32).astype(BF)
    d_all = d_got.reshape(n_tp, count, -1)

    def hidden(d, low_all):
        return jnp.einsum("tkr,kc->trc", d, low_all, preferred_element_type=F32)

    term = hidden(d_all[:, :, :ff_blk], every_gate_low) + hidden(
        d_all[:, :, ff_blk : 2 * ff_blk], every_up_low
    )
    term = term.astype(BF).reshape(n_tp, ff_blk, group, fs_own).transpose(0, 2, 1, 3)
    big_send = fit(term, (n_tp, group, ff_blk, up_to(fs_own, 128)))

    small_term = contract_rows(every_narrow, low_got.reshape(count, -1)).astype(BF)
    small_send = small_term.reshape(n_dp, small // n_dp, -1)
    big_got, small_got, _ = exchange(
        functools.partial(second_exchange, n_dp, n_tp),
        1,
        (big_send, small_send),
        [
            jax.ShapeDtypeStruct((n_dp,) + big_send.shape[2:], BF),
            jax.ShapeDtypeStruct(small_send.shape, BF),
            jax.ShapeDtypeStruct(big_send.shape, BF),
        ],
        [(n_tp, group), (n_tp, group), (n_dp,), (n_dp,), (n_dp,), (n_dp,), (2,)],
    )
    grad_width_hidden = (
        big_got.reshape(n_dp * ff_blk, -1)[:ff_part, :fs_own].astype(F32)
    )

    def small_out(start):
        part = small_got[:, :, start : start + fs_blk].transpose(1, 0, 2)
        return part.reshape(small // n_dp, n_dp * fs_blk)[:, :fs_part].astype(F32)

    grad_width_in = contract_rows(tok_got.reshape(count, -1), every_d_narrow)
    return (grad_width_in, small_out(0), small_out(fs_blk), grad_width_hidden)


def solution(mesh):
    return jax.shard_map(
        functools.partial(on_device, mesh.shape["dp"], mesh.shape["tensor"]),
        mesh=mesh,
        in_specs=(
            P(("dp", "tensor"), None),
            P("dp", "tensor"),
            P(None, "tensor"),
            P(None, "tensor"),
            P(None, "tensor"),
            P("tensor", None),
        ),
        out_specs=(P("dp", "tensor"), P("dp", "tensor"), P("dp", "tensor"), P("tensor", "dp")),
        check_vma=False,
    )
```
